32 devices in a mesh: parts: 2 (over y), ctx: 4 (over z), wt: 2 (over x), sub: 2 (over core).
Axes of the slice: x: 2, y: 2, z: 4, core: 2. Of those that a mesh axis runs over, the one named last changes fastest.
Arguments:
- tokens: bfloat16 [2048, 4096], P(('parts', 'ctx', 'wt')), parts along dimension 0, may hold values from -6 to 6
- block_order: int32 [32], P('parts'), parts along dimension 0, may hold values from 0 to 15, each once
- q_weight: bfloat16 [4096, 2048], P('wt', 'sub')
- key_value_weight: bfloat16 [4096, 4, 2, 128], P('wt', 'sub'), may hold values from -0.09375 to 0.09375
- out_weight: bfloat16 [2048, 4096], P('sub', 'wt'), may hold values from -0.5 to 0.5
Outputs:
- attended: bfloat16 [2048, 4096], P(('parts', 'ctx', 'wt'), 'sub'), parts along dimension 0
The draws below stay inside these ranges and needn't reach their ends.
There are 2 independent parts, one for each index of `parts`. The reference program is written for one: setup_inputs(seed, part) draws one part's arguments, and reference() takes and returns one part's arrays. A program takes and returns all parts, laid end to end along the dimension named above; an argument that names none is the same for every part. Nothing has to cross between parts.
Inputs may be any that keep to these rules, and one draw needn't show every extreme that they name: block_order is a permutation of the 16 block numbers.
All inputs are finite; a program needn't handle non-finite values.
Results may differ from the reference program's by a relative error of at most 0.014.
The reference program's roundings to bfloat16 on the way count: a program that leaves them out, or rounds other values in their place, can miss the bound.
Values may be sent and summed in bfloat16 or wider, within the bound.
A program may use at most 128 MiB of HBM per device.

```python
import jax
import jax.numpy as jnp
from jax import lax

MODEL_WIDTH = 4096
HEAD_SIZE = 128
HQ = 16
KEY_VALUE_HEADS = 4
GROUP = 4
BLOCK = 64
NBLK = 16
DOCUMENT_TOKENS = 1024


def draw_q_weight(key, part):
    base = jax.random.normal(key, (MODEL_WIDTH, HQ * HEAD_SIZE), jnp.float32) * MODEL_WIDTH ** (-0.5)
    return base.astype(jnp.bfloat16)


def block_scale(rng, dims, split, low, largest):
    level, own = 1.0, jax.random.fold_in(rng, 6)
    for position, blocks in split:
        heights = jnp.exp(jax.random.uniform(jax.random.fold_in(own, position), (blocks,), jnp.float32, low / len(split), largest / len(split)))
        level = level * jnp.repeat(heights, dims[position] // blocks).reshape([-1 if axis == position else 1 for axis in range(len(dims))])
    return level


def centred(stream_key, dims, spread, limit, cuts=(), held_as=jnp.bfloat16):
    drawn = spread * jax.random.normal(stream_key, dims, jnp.float32)
    if cuts:
        drawn = drawn * block_scale(stream_key, dims, cuts, -0.22, 0.18)
    return jnp.clip(drawn, -limit, limit).astype(held_as)


def setup_inputs(seed: int = 0, part: int = 0) -> dict:
    seeds = jax.random.split(jax.random.key(seed), 6)
    own_keys = jax.random.split(jax.random.fold_in(seeds[5], part), 6)
    return {
        "tokens": centred(own_keys[0], (DOCUMENT_TOKENS, MODEL_WIDTH), 1.0, 6.0, ((0, 8),)),
        "block_order": jax.random.permutation(own_keys[1], NBLK).astype(jnp.int32),
        "q_weight": draw_q_weight(jax.random.fold_in(seeds[5], 71), part),
        "key_value_weight": centred(seeds[3], (MODEL_WIDTH, KEY_VALUE_HEADS, 2, HEAD_SIZE), MODEL_WIDTH ** -0.5, 0.09375, ((0, 2), (1, 2))),
        "out_weight": centred(seeds[4], (HQ * HEAD_SIZE, MODEL_WIDTH), HEAD_SIZE ** -0.5, 0.5, ((0, 2), (1, 2))),
    }


rope_base = 500000.0
epsilon = 1e-05

def rotary(values_in, positions):
    half_dim = HEAD_SIZE // 2
    inverse_freq = rope_base ** (-(jnp.arange(half_dim, dtype=jnp.float32) * 2.0 / HEAD_SIZE))
    angles = positions.astype(jnp.float32)[:, None] * inverse_freq[None, :]
    cosine = jnp.concatenate([jnp.cos(angles), jnp.cos(angles)], axis=1)[:, None, :]
    sine = jnp.concatenate([jnp.sin(angles), jnp.sin(angles)], axis=1)[:, None, :]
    rotated = jnp.concatenate([-values_in[..., half_dim:], values_in[..., :half_dim]], axis=-1)
    return values_in * cosine + rotated * sine

def reference(tokens, block_order, q_weight, key_value_weight, out_weight):
    row_ids = jnp.arange(DOCUMENT_TOKENS, dtype=jnp.int32)
    positions = jnp.take(block_order, row_ids // BLOCK).astype(jnp.int32) * BLOCK + row_ids % BLOCK
    widened = tokens.astype(jnp.float32)
    normalized_input = (widened * lax.rsqrt(lax.optimization_barrier(jnp.mean(widened * widened, axis=1, keepdims=True)) + epsilon)).astype(jnp.bfloat16)
    queries = jnp.dot(normalized_input, q_weight, preferred_element_type=jnp.float32).reshape(DOCUMENT_TOKENS, HQ, HEAD_SIZE)
    key_value_rows = jnp.dot(normalized_input, key_value_weight.reshape(MODEL_WIDTH, KEY_VALUE_HEADS * 2 * HEAD_SIZE), preferred_element_type=jnp.float32).reshape(DOCUMENT_TOKENS, KEY_VALUE_HEADS, 2, HEAD_SIZE)
    q_rot = rotary(queries, positions).astype(jnp.bfloat16)
    k_rot = rotary(key_value_rows[:, :, 0, :], positions).astype(jnp.bfloat16)
    values = key_value_rows[:, :, 1, :].astype(jnp.bfloat16)
    q_heads = jnp.transpose(q_rot, (1, 0, 2))
    k_heads = jnp.repeat(jnp.transpose(k_rot, (1, 0, 2)), GROUP, axis=0)
    v_heads = jnp.repeat(jnp.transpose(values, (1, 0, 2)), GROUP, axis=0)
    visible = positions[:, None] >= positions[None, :]
    score_factor = 1.0 / HEAD_SIZE ** 0.5

    def one_head(head_inputs):
        query_rows, key_rows, value_rows = head_inputs
        scores = jnp.dot(query_rows, key_rows.T, preferred_element_type=jnp.float32) * score_factor
        scores = jnp.where(visible, scores, -1e+30)
        row_max = lax.optimization_barrier(jnp.max(scores, axis=1, keepdims=True))
        weights = jnp.where(visible, jnp.exp(scores - row_max), 0.0)
        row_total = lax.optimization_barrier(jnp.sum(weights, axis=1, keepdims=True))
        mixed = jnp.dot(weights.astype(jnp.bfloat16), value_rows, preferred_element_type=jnp.float32)
        return mixed / row_total
    heads_out = lax.map(one_head, (q_heads, k_heads, v_heads))
    heads_out = jnp.transpose(heads_out, (1, 0, 2)).reshape(DOCUMENT_TOKENS, HQ * HEAD_SIZE).astype(jnp.bfloat16)
    return jnp.dot(heads_out, out_weight, preferred_element_type=jnp.float32).astype(jnp.bfloat16)
```

```python
import functools

import jax
import jax.numpy as jnp
from jax import lax
from jax.experimental import pallas as pl
from jax.experimental.pallas import tpu as pltpu
from jax.sharding import PartitionSpec as P

MESH = pl.DeviceIdType.MESH

rope_base = 500000.0
epsilon = 1e-05


def token_positions(row_ids, block_order, block_len):
    number = block_order.shape[0]
    blocks = row_ids // block_len
    equal = blocks[:, None] == jnp.arange(number, dtype=jnp.int32)[None, :]
    chosen = jnp.sum(jnp.where(equal, block_order[None, :], 0), axis=1)
    return chosen * block_len + row_ids % block_len


def rotary(values_in, positions, head_dim):
    half_dim = head_dim // 2
    inverse_freq = rope_base ** (-(jnp.arange(half_dim, dtype=jnp.float32) * 2.0 / head_dim))
    angles = positions.astype(jnp.float32)[:, None] * inverse_freq[None, :]
    cosine = jnp.concatenate([jnp.cos(angles), jnp.cos(angles)], axis=1)[:, None, :]
    sine = jnp.concatenate([jnp.sin(angles), jnp.sin(angles)], axis=1)[:, None, :]
    rotated = jnp.concatenate([-values_in[..., half_dim:], values_in[..., :half_dim]], axis=-1)
    return values_in * cosine + rotated * sine


def body(tokens, block_order, q_weight, key_value_weight, out_weight):
    tok_rows = tokens.shape[0]
    block_len = tok_rows // 2
    head_dim = key_value_weight.shape[3]
    kv_local = key_value_weight.shape[1]
    q_cols = q_weight.shape[1]
    q_local = q_cols // head_dim
    group = q_local // kv_local
    kv_cols = kv_local * 2 * head_dim
    kv_flat = key_value_weight.reshape(key_value_weight.shape[0], kv_cols)
    own_first = lax.axis_index(("ctx", "wt")) * tok_rows
    own_ids = own_first + jnp.arange(tok_rows, dtype=jnp.int32)
    own_positions = token_positions(own_ids, block_order, block_len)
    widened = tokens.astype(jnp.float32)
    normalized_input = (
        widened * lax.rsqrt(jnp.mean(widened * widened, axis=1, keepdims=True) + epsilon)
    ).astype(jnp.bfloat16)
    queries = jnp.dot(
        normalized_input,
        lax.all_gather(q_weight, "wt", axis=0, tiled=True),
        preferred_element_type=jnp.float32,
    )
    key_value_rows = jnp.dot(
        normalized_input,
        lax.all_gather(kv_flat, "wt", axis=0, tiled=True),
        preferred_element_type=jnp.float32,
    )
    queries = queries.reshape(tok_rows, q_local, head_dim)
    key_value_rows = key_value_rows.reshape(tok_rows, kv_local, 2, head_dim)
    q_rot = rotary(queries, own_positions, head_dim).astype(jnp.bfloat16)
    k_rot = rotary(key_value_rows[:, :, 0, :], own_positions, head_dim).astype(jnp.bfloat16)
    value_rows = key_value_rows[:, :, 1, :].astype(jnp.bfloat16)
    q_grouped = jnp.transpose(q_rot.reshape(tok_rows, kv_local, group, head_dim), (1, 2, 0, 3))
    q_grouped = q_grouped.reshape(kv_local, group * tok_rows, head_dim)
    query_positions = jnp.tile(own_positions, group)
    score_factor = 1.0 / head_dim**0.5
    key_part = lax.all_gather(k_rot, ("ctx", "wt"), axis=0, tiled=True)
    value_part = lax.all_gather(value_rows, ("ctx", "wt"), axis=0, tiled=True)
    count = key_part.shape[0]
    key_ids = jnp.arange(count, dtype=jnp.int32)
    key_positions = token_positions(key_ids, block_order, block_len)
    visible = query_positions[:, None] >= key_positions[None, :]
    old_max = jnp.full((kv_local, group * tok_rows), -1e30, jnp.float32)
    scores = (
        jnp.einsum("hqd,khd->hqk", q_grouped, key_part, preferred_element_type=jnp.float32)
        * score_factor
    )
    scores = jnp.where(visible[None], scores, -1e30)
    new_max = jnp.maximum(old_max, jnp.max(scores, axis=2))
    weights = jnp.where(visible[None], jnp.exp(scores - new_max[..., None]), 0.0)
    new_total = jnp.sum(weights, axis=2)
    new_acc = jnp.einsum(
        "hqk,khd->hqd", weights.astype(jnp.bfloat16), value_part, preferred_element_type=jnp.float32
    )
    heads_out = new_acc / new_total[..., None]
    heads_out = jnp.transpose(heads_out.reshape(kv_local, group, tok_rows, head_dim), (2, 0, 1, 3))
    heads_out = heads_out.reshape(tok_rows, q_cols).astype(jnp.bfloat16)
    partial_out = jnp.dot(
        heads_out,
        lax.all_gather(out_weight, "wt", axis=1, tiled=True),
        preferred_element_type=jnp.float32,
    )
    return lax.psum_scatter(
        partial_out.astype(jnp.bfloat16), "sub", scatter_dimension=1, tiled=True
    )


OUT_CHUNKS = 4
ROW_CHUNKS = 2


def fused_kernel(
    n,
    tokens,
    cosine,
    sine,
    q_pos,
    k_pos,
    q_hbm,
    kv_hbm,
    o_hbm,
    out,
    q_w,
    kv_raw,
    kv_wide,
    kv_w,
    o_w,
    x_own,
    x_send,
    x_recv,
    pkv_send,
    pkv_recv,
    pq_send,
    pq_recv,
    kv_keep,
    q_keep,
    q_rot,
    kv_all,
    heads,
    o_keep,
    o_send,
    o_recv,
    o_fin,
    o_last,
    load_sem,
    xs_sem,
    xr_sem,
    fs_sem,
    fr_sem,
    ps_sem,
    pr_sem,
    zs_sem,
    zr_sem,
    hs_sem,
    hr_sem,
    os_sem,
    or_sem,
    ls_sem,
    lr_sem,
):
    c = lax.axis_index("ctx")
    w = lax.axis_index("wt")
    s = lax.axis_index("sub")
    rows, width = tokens.shape
    feats = width // 2
    part = feats // 2
    hd = 128
    q_half = q_w.shape[2]
    heads_here = q_half // hd
    partner = {"wt": 1 - w}
    sibling = {"sub": 1 - s}
    across = {"wt": 1 - w, "sub": 1 - s}

    loads = [
        pltpu.make_async_copy(kv_hbm, kv_raw, load_sem.at[0]),
        pltpu.make_async_copy(
            q_hbm.at[:, pl.ds(pl.multiple_of((1 - w) * q_half, q_half), q_half)],
            q_w.at[0],
            load_sem.at[1],
        ),
        pltpu.make_async_copy(
            q_hbm.at[:, pl.ds(pl.multiple_of(w * q_half, q_half), q_half)],
            q_w.at[1],
            load_sem.at[2],
        ),
        pltpu.make_async_copy(o_hbm, o_w, load_sem.at[3]),
    ]
    for load in loads:
        load.start()

    barrier = pltpu.get_barrier_semaphore()
    for target in (partner, sibling, across):
        pl.semaphore_signal(barrier, inc=1, device_id=target, device_id_type=MESH)

    @pl.when(c > 0)
    def _():
        pl.semaphore_signal(barrier, inc=1, device_id={"ctx": c - 1}, device_id_type=MESH)

    @pl.when(c < n - 1)
    def _():
        pl.semaphore_signal(barrier, inc=1, device_id={"ctx": c + 1}, device_id_type=MESH)

    step = 16
    chunk = rows // ROW_CHUNKS
    own_at = pl.multiple_of(w * feats, feats)
    send_at = pl.multiple_of((1 - w) * feats + s * part, part)

    def normalise(i, carry):
        at = pl.ds(pl.multiple_of(i * step, step), step)
        whole = tokens[at, :].astype(jnp.float32)
        scale = lax.rsqrt(jnp.mean(whole * whole, axis=1, keepdims=True) + epsilon)
        x_send[at, :] = (tokens[at, pl.ds(send_at, part)].astype(jnp.float32) * scale).astype(
            jnp.bfloat16
        )
        x_own[at, :] = (tokens[at, pl.ds(own_at, feats)].astype(jnp.float32) * scale).astype(
            jnp.bfloat16
        )
        return carry

    x_copies = []
    for j in range(ROW_CHUNKS):
        lax.fori_loop(j * (chunk // step), (j + 1) * (chunk // step), normalise, 0)
        if j == 0:
            pl.semaphore_wait(
                barrier, 3 + jnp.minimum(c, 1) + jnp.minimum(n - 1 - c, 1)
            )

        copy = pltpu.make_async_remote_copy(
            src_ref=x_send.at[pl.ds(j * chunk, chunk)],
            dst_ref=x_recv.at[s, pl.ds(j * chunk, chunk)],
            send_sem=xs_sem.at[j],
            recv_sem=xr_sem.at[j],
            device_id=partner,
            device_id_type=MESH,
        )
        copy.start()
        x_copies.append(copy)

    loads[0].wait()
    kv_wide[...] = kv_raw[...].astype(jnp.float32)
    for h in range(2):
        for t in range(2):
            kv_w[h, :, t * hd : (t + 1) * hd] = kv_wide[
                pl.ds(h * 2 + t, feats, stride=4), :
            ].astype(jnp.bfloat16)

    def send_part(index, src, dst, block):
        copy = pltpu.make_async_remote_copy(
            src_ref=src.at[block],
            dst_ref=dst.at[block],
            send_sem=ps_sem.at[index],
            recv_sem=pr_sem.at[index],
            device_id=partner,
            device_id_type=MESH,
        )
        copy.start()
        return copy

    f32 = jnp.float32
    own = x_own[...]
    pkv_send[w] = jnp.dot(own, kv_w[1 - w], preferred_element_type=f32).astype(jnp.bfloat16)
    parts = [send_part(0, pkv_send, pkv_recv, w)]
    loads[1].wait()
    pq_send[w] = jnp.dot(own, q_w[0], preferred_element_type=f32).astype(jnp.bfloat16)
    parts.append(send_part(1, pq_send, pq_recv, w))

    forwards = []
    for j in range(ROW_CHUNKS):
        x_copies[j].wait_recv()
        copy = pltpu.make_async_remote_copy(
            src_ref=x_recv.at[s, pl.ds(j * chunk, chunk)],
            dst_ref=x_recv.at[s, pl.ds(j * chunk, chunk)],
            send_sem=fs_sem.at[j],
            recv_sem=fr_sem.at[j],
            device_id=sibling,
            device_id_type=MESH,
        )
        copy.start()
        forwards.append(copy)
    kv_keep[w] = jnp.dot(own, kv_w[w], preferred_element_type=f32)
    for copy in forwards:
        copy.wait()

    def other(weight):
        return jnp.dot(x_recv[0], weight[:part], preferred_element_type=f32) + jnp.dot(
            x_recv[1], weight[part:], preferred_element_type=f32
        )

    pkv_send[1 - w] = other(kv_w[1 - w]).astype(jnp.bfloat16)
    parts.append(send_part(2, pkv_send, pkv_recv, 1 - w))
    pq_send[1 - w] = other(q_w[0]).astype(jnp.bfloat16)
    parts.append(send_part(3, pq_send, pq_recv, 1 - w))
    kv_keep[1 - w] = other(kv_w[w])

    def rotate(t, block):
        turned = pltpu.roll(t, hd // 2, 1)
        return (t * cosine[block] + turned * sine[block]).astype(jnp.bfloat16)

    def z_copy(way, t, b):
        block = c - t if way == 0 else c + t
        at = pl.ds(pl.multiple_of(block * 2 * rows + b * rows, rows), rows)
        return pltpu.make_async_remote_copy(
            src_ref=kv_all.at[at],
            dst_ref=kv_all.at[at],
            send_sem=zs_sem.at[way, t, b],
            recv_sem=zr_sem.at[way, t, b],
            device_id={"ctx": c + 1 if way == 0 else c - 1},
            device_id_type=MESH,
        )

    def z_sends(way, t):
        if way == 0:
            return jnp.logical_and(c - t >= 0, c < n - 1)
        return jnp.logical_and(c + t <= n - 1, c > 0)

    def z_gets(way, t):
        return c - 1 - t >= 0 if way == 0 else c + 1 + t <= n - 1

    for order, index in ((1, 0), (0, 2)):
        parts[index].wait_recv()
        b = jnp.where(order == 0, w, 1 - w)
        kv = kv_keep[b] + pkv_recv[b].astype(f32)
        at = pl.ds(pl.multiple_of(c * 2 * rows + b * rows, rows), rows)
        kv_all[at, :hd] = rotate(kv[:, :hd], b)
        kv_all[at, hd:] = kv[:, hd:].astype(jnp.bfloat16)
        for way in range(2):

            @pl.when(z_sends(way, 0))
            def _():
                z_copy(way, 0, b).start()

    loads[2].wait()
    q_keep[w] = jnp.dot(own, q_w[1], preferred_element_type=f32)
    q_keep[1 - w] = other(q_w[1])

    for t in range(n - 1):
        for order in (1, 0):
            b = jnp.where(order == 0, w, 1 - w)
            for way in range(2):

                @pl.when(z_gets(way, t))
                def _():
                    z_copy(way, t, b).wait_recv()

                if t < n - 2:

                    @pl.when(z_sends(way, t + 1))
                    def _():
                        z_copy(way, t + 1, b).start()

    for order, index in ((1, 1), (0, 3)):
        parts[index].wait_recv()
        b = jnp.where(order == 0, w, 1 - w)
        q = q_keep[b] + pq_recv[b].astype(f32)
        at = pl.ds(pl.multiple_of(b * rows, rows), rows)
        for h in range(heads_here):
            q_rot[h, at, :] = rotate(q[:, h * hd : (h + 1) * hd], b)

    h_copies = []
    factor = 1.0 / hd**0.5
    for h in range(heads_here):
        visible = q_pos[...] >= k_pos[...]
        scores = (
            lax.dot_general(
                q_rot[h], kv_all[:, :hd], (((1,), (1,)), ((), ())), preferred_element_type=f32
            )
            * factor
        )
        scores = jnp.where(visible, scores, -1e30)
        top = jnp.max(scores, axis=1, keepdims=True)
        weights = jnp.where(visible, jnp.exp(scores - top), 0.0)
        total = jnp.sum(weights, axis=1, keepdims=True)
        mixed = jnp.dot(weights.astype(jnp.bfloat16), kv_all[:, hd:], preferred_element_type=f32)
        heads[w, h // 2, :, (h % 2) * hd : (h % 2 + 1) * hd] = (mixed / total).astype(jnp.bfloat16)
        place = heads.at[w, h // 2, :, pl.ds((h % 2) * hd, hd)]
        copy = pltpu.make_async_remote_copy(
            src_ref=place,
            dst_ref=place,
            send_sem=hs_sem.at[h],
            recv_sem=hr_sem.at[h],
            device_id=partner,
            device_id_type=MESH,
        )
        copy.start()
        h_copies.append(copy)
    loads[3].wait()
    for copy in h_copies:
        copy.wait_recv()

    span = o_w.shape[1] // OUT_CHUNKS

    def project(block, j):
        at = pl.ds(pl.multiple_of(block * rows, rows), rows)
        total = None
        for g in range(2):
            for p in range(heads_here // 2):
                first = (g * (heads_here // 2) + p) * 2 * hd
                term = jnp.dot(
                    heads[g, p, at, :],
                    o_w[first : first + 2 * hd, j * span : (j + 1) * span],
                    preferred_element_type=f32,
                )
                total = term if total is None else total + term
        return total

    def o_copy(j):
        return pltpu.make_async_remote_copy(
            src_ref=o_send.at[j],
            dst_ref=o_recv.at[j],
            send_sem=os_sem.at[j],
            recv_sem=or_sem.at[j],
            device_id=sibling,
            device_id_type=MESH,
        )

    def last_copy(j):
        return pltpu.make_async_remote_copy(
            src_ref=o_fin.at[j],
            dst_ref=o_last.at[j],
            send_sem=ls_sem.at[j],
            recv_sem=lr_sem.at[j],
            device_id=across,
            device_id_type=MESH,
        )

    for j in range(OUT_CHUNKS):
        o_keep[...] = project(1 - w, j)

        @pl.when(s == w)
        def _():
            o_send[j] = o_keep[...].astype(jnp.bfloat16)
            o_copy(j).start()

        @pl.when(s != w)
        def _():
            o_copy(j).wait_recv()
            o_fin[j] = (o_keep[...] + o_recv[j].astype(f32)).astype(jnp.bfloat16)
            last_copy(j).start()

    for j in range(OUT_CHUNKS):
        o_keep[...] = project(w, j)

        @pl.when(s != w)
        def _():
            o_send[j] = o_keep[...].astype(jnp.bfloat16)
            o_copy(j).start()

        @pl.when(s == w)
        def _():
            o_copy(j).wait_recv()
            out[:, j * span : (j + 1) * span] = (o_keep[...] + o_recv[j].astype(f32)).astype(
                jnp.bfloat16
            )

    for j in range(OUT_CHUNKS):

        @pl.when(s != w)
        def _():
            last_copy(j).wait()
            out[:, j * span : (j + 1) * span] = o_last[j]

        o_copy(j).wait_send()

    for copy in x_copies + parts + h_copies:
        copy.wait_send()
    for t in range(n - 1):
        for order in (1, 0):
            b = jnp.where(order == 0, w, 1 - w)
            for way in range(2):

                @pl.when(z_sends(way, t))
                def _():
                    z_copy(way, t, b).wait_send()


def fused_body(n, tokens, block_order, q_weight, key_value_weight, out_weight):
    rows, width = tokens.shape
    feats, kv_local, _, hd = key_value_weight.shape
    q_half = q_weight.shape[1] // 2
    block_len = rows // 2
    first = lax.axis_index("ctx") * 2 * rows
    own_positions = token_positions(
        first + jnp.arange(2 * rows, dtype=jnp.int32), block_order, block_len
    )
    key_positions = token_positions(
        jnp.arange(2 * rows * n, dtype=jnp.int32), block_order, block_len
    )
    half = hd // 2
    inverse_freq = rope_base ** (-(jnp.arange(half, dtype=jnp.float32) * 2.0 / hd))
    angles = own_positions.astype(jnp.float32)[:, None] * inverse_freq[None, :]
    cosine = jnp.concatenate([jnp.cos(angles), jnp.cos(angles)], axis=1).reshape(2, rows, hd)
    sine = jnp.concatenate([-jnp.sin(angles), jnp.sin(angles)], axis=1).reshape(2, rows, hd)
    bf16, f32 = jnp.bfloat16, jnp.float32
    span = out_weight.shape[1] // OUT_CHUNKS
    here = q_half // hd
    dma = pltpu.SemaphoreType.DMA
    vmem = pl.BlockSpec(memory_space=pltpu.VMEM)
    hbm = pl.BlockSpec(memory_space=pl.ANY)
    return pl.pallas_call(
        functools.partial(fused_kernel, n),
        out_shape=jax.ShapeDtypeStruct((rows, out_weight.shape[1]), bf16),
        in_specs=[vmem] * 5 + [hbm] * 3,
        out_specs=vmem,
        scratch_shapes=[
            pltpu.VMEM((2, feats, q_half), bf16),
            pltpu.VMEM((feats * kv_local * 2, hd), bf16),
            pltpu.VMEM((feats * kv_local * 2, hd), f32),
            pltpu.VMEM((2, feats, 2 * hd), bf16),
            pltpu.VMEM(out_weight.shape, bf16),
            pltpu.VMEM((rows, feats), bf16),
            pltpu.VMEM((rows, feats // 2), bf16),
            pltpu.VMEM((2, rows, feats // 2), bf16),
            pltpu.VMEM((2, rows, 2 * hd), bf16),
            pltpu.VMEM((2, rows, 2 * hd), bf16),
            pltpu.VMEM((2, rows, q_half), bf16),
            pltpu.VMEM((2, rows, q_half), bf16),
            pltpu.VMEM((2, rows, 2 * hd), f32),
            pltpu.VMEM((2, rows, q_half), f32),
            pltpu.VMEM((here, 2 * rows, hd), bf16),
            pltpu.VMEM((n * 2 * rows, 2 * hd), bf16),
            pltpu.VMEM((2, here // 2, 2 * rows, 2 * hd), bf16),
            pltpu.VMEM((rows, span), f32),
            pltpu.VMEM((OUT_CHUNKS, rows, span), bf16),
            pltpu.VMEM((OUT_CHUNKS, rows, span), bf16),
            pltpu.VMEM((OUT_CHUNKS, rows, span), bf16),
            pltpu.VMEM((OUT_CHUNKS, rows, span), bf16),
            dma((4,)),
            dma((ROW_CHUNKS,)),
            dma((ROW_CHUNKS,)),
            dma((ROW_CHUNKS,)),
            dma((ROW_CHUNKS,)),
            dma((4,)),
            dma((4,)),
            dma((2, n - 1, 2)),
            dma((2, n - 1, 2)),
            dma((here,)),
            dma((here,)),
            dma((OUT_CHUNKS,)),
            dma((OUT_CHUNKS,)),
            dma((OUT_CHUNKS,)),
            dma((OUT_CHUNKS,)),
        ],
        compiler_params=pltpu.CompilerParams(
            collective_id=0, has_side_effects=True, vmem_limit_bytes=56 * 1024 * 1024
        ),
    )(
        tokens,
        cosine,
        sine,
        own_positions[:, None],
        key_positions[None, :],
        q_weight,
        key_value_weight.reshape(feats * kv_local * 2, hd),
        out_weight,
    )


def solution(mesh):
    in_specs = (
        P(("parts", "ctx", "wt"), None),
        P("parts"),
        P("wt", "sub"),
        P("wt", "sub", None, None),
        P("sub", "wt"),
    )
    out_specs = P(("parts", "ctx", "wt"), "sub")
    n = mesh.shape["ctx"]
    fits = mesh.shape["wt"] == 2 and mesh.shape["sub"] == 2 and 1 < n <= 8
    run = functools.partial(fused_body, n) if fits else body
    return jax.shard_map(run, mesh=mesh, in_specs=in_specs, out_specs=out_specs, check_vma=False)
```

```python
import functools

import jax
import jax.numpy as jnp
import numpy as np
from jax import lax
from jax.experimental import pallas as pl
from jax.experimental.pallas import tpu as pltpu
from jax.sharding import PartitionSpec as P

MESH = pl.DeviceIdType.MESH

rope_base = 500000.0
epsilon = 1e-05


def token_positions(row_ids, block_order, block_len):
    number = block_order.shape[0]
    blocks = row_ids // block_len
    equal = blocks[:, None] == jnp.arange(number, dtype=jnp.int32)[None, :]
    chosen = jnp.sum(jnp.where(equal, block_order[None, :], 0), axis=1)
    return chosen * block_len + row_ids % block_len


def rotary(values_in, positions, head_dim):
    half_dim = head_dim // 2
    inverse_freq = rope_base ** (-(jnp.arange(half_dim, dtype=jnp.float32) * 2.0 / head_dim))
    angles = positions.astype(jnp.float32)[:, None] * inverse_freq[None, :]
    cosine = jnp.concatenate([jnp.cos(angles), jnp.cos(angles)], axis=1)[:, None, :]
    sine = jnp.concatenate([jnp.sin(angles), jnp.sin(angles)], axis=1)[:, None, :]
    rotated = jnp.concatenate([-values_in[..., half_dim:], values_in[..., :half_dim]], axis=-1)
    return values_in * cosine + rotated * sine


def body(tokens, block_order, q_weight, key_value_weight, out_weight):
    tok_rows = tokens.shape[0]
    block_len = tok_rows // 2
    head_dim = key_value_weight.shape[3]
    kv_local = key_value_weight.shape[1]
    q_cols = q_weight.shape[1]
    q_local = q_cols // head_dim
    group = q_local // kv_local
    kv_cols = kv_local * 2 * head_dim
    kv_flat = key_value_weight.reshape(key_value_weight.shape[0], kv_cols)
    own_first = lax.axis_index(("ctx", "wt")) * tok_rows
    own_ids = own_first + jnp.arange(tok_rows, dtype=jnp.int32)
    own_positions = token_positions(own_ids, block_order, block_len)
    widened = tokens.astype(jnp.float32)
    normalized_input = (
        widened * lax.rsqrt(jnp.mean(widened * widened, axis=1, keepdims=True) + epsilon)
    ).astype(jnp.bfloat16)
    queries = jnp.dot(
        normalized_input,
        lax.all_gather(q_weight, "wt", axis=0, tiled=True),
        preferred_element_type=jnp.float32,
    )
    key_value_rows = jnp.dot(
        normalized_input,
        lax.all_gather(kv_flat, "wt", axis=0, tiled=True),
        preferred_element_type=jnp.float32,
    )
    queries = queries.reshape(tok_rows, q_local, head_dim)
    key_value_rows = key_value_rows.reshape(tok_rows, kv_local, 2, head_dim)
    q_rot = rotary(queries, own_positions, head_dim).astype(jnp.bfloat16)
    k_rot = rotary(key_value_rows[:, :, 0, :], own_positions, head_dim).astype(jnp.bfloat16)
    value_rows = key_value_rows[:, :, 1, :].astype(jnp.bfloat16)
    q_grouped = jnp.transpose(q_rot.reshape(tok_rows, kv_local, group, head_dim), (1, 2, 0, 3))
    q_grouped = q_grouped.reshape(kv_local, group * tok_rows, head_dim)
    query_positions = jnp.tile(own_positions, group)
    score_factor = 1.0 / head_dim**0.5
    key_part = lax.all_gather(k_rot, ("ctx", "wt"), axis=0, tiled=True)
    value_part = lax.all_gather(value_rows, ("ctx", "wt"), axis=0, tiled=True)
    count = key_part.shape[0]
    key_ids = jnp.arange(count, dtype=jnp.int32)
    key_positions = token_positions(key_ids, block_order, block_len)
    visible = query_positions[:, None] >= key_positions[None, :]
    old_max = jnp.full((kv_local, group * tok_rows), -1e30, jnp.float32)
    scores = (
        jnp.einsum("hqd,khd->hqk", q_grouped, key_part, preferred_element_type=jnp.float32)
        * score_factor
    )
    scores = jnp.where(visible[None], scores, -1e30)
    new_max = jnp.maximum(old_max, jnp.max(scores, axis=2))
    weights = jnp.where(visible[None], jnp.exp(scores - new_max[..., None]), 0.0)
    new_total = jnp.sum(weights, axis=2)
    new_acc = jnp.einsum(
        "hqk,khd->hqd", weights.astype(jnp.bfloat16), value_part, preferred_element_type=jnp.float32
    )
    heads_out = new_acc / new_total[..., None]
    heads_out = jnp.transpose(heads_out.reshape(kv_local, group, tok_rows, head_dim), (2, 0, 1, 3))
    heads_out = heads_out.reshape(tok_rows, q_cols).astype(jnp.bfloat16)
    partial_out = jnp.dot(
        heads_out,
        lax.all_gather(out_weight, "wt", axis=1, tiled=True),
        preferred_element_type=jnp.float32,
    )
    return lax.psum_scatter(
        partial_out.astype(jnp.bfloat16), "sub", scatter_dimension=1, tiled=True
    )


OUT_CHUNKS = 4
ROW_CHUNKS = 4


def fused_kernel(
    n,
    token_hbm,
    order,
    freq,
    q_hbm,
    kv_hbm,
    o_hbm,
    out,
    tokens,
    cosine,
    sine,
    q_w,
    kv_raw,
    kv_wide,
    kv_w,
    o_w,
    x_own,
    x_send,
    x_recv,
    pkv_send,
    pkv_recv,
    pq_send,
    pq_recv,
    kv_keep,
    q_keep,
    q_rot,
    kv_all,
    heads,
    o_keep,
    o_send,
    o_recv,
    o_fin,
    o_last,
    token_sem,
    load_sem,
    xs_sem,
    xr_sem,
    fs_sem,
    fr_sem,
    ps_sem,
    pr_sem,
    zs_sem,
    zr_sem,
    hs_sem,
    hr_sem,
    os_sem,
    or_sem,
    ls_sem,
    lr_sem,
):
    c = lax.axis_index("ctx")
    w = lax.axis_index("wt")
    s = lax.axis_index("sub")
    rows, width = tokens.shape
    feats = width // 2
    part = feats // 2
    hd = 128
    q_half = q_w.shape[2]
    heads_here = q_half // hd
    partner = {"wt": 1 - w}
    sibling = {"sub": 1 - s}
    across = {"wt": 1 - w, "sub": 1 - s}

    chunk = rows // ROW_CHUNKS
    token_loads = [
        pltpu.make_async_copy(
            token_hbm.at[pl.ds(j * chunk, chunk)],
            tokens.at[pl.ds(j * chunk, chunk)],
            token_sem.at[j],
        )
        for j in range(ROW_CHUNKS)
    ]
    for load in token_loads:
        load.start()
    loads = [
        pltpu.make_async_copy(kv_hbm, kv_raw, load_sem.at[0]),
        pltpu.make_async_copy(
            q_hbm.at[:, pl.ds(pl.multiple_of((1 - w) * q_half, q_half), q_half)],
            q_w.at[0],
            load_sem.at[1],
        ),
        pltpu.make_async_copy(
            q_hbm.at[:, pl.ds(pl.multiple_of(w * q_half, q_half), q_half)],
            q_w.at[1],
            load_sem.at[2],
        ),
        pltpu.make_async_copy(o_hbm, o_w, load_sem.at[3]),
    ]
    for load in loads:
        load.start()

    barrier = pltpu.get_barrier_semaphore()
    for target in (partner, sibling, across):
        pl.semaphore_signal(barrier, inc=1, device_id=target, device_id_type=MESH)

    @pl.when(c > 0)
    def _():
        pl.semaphore_signal(barrier, inc=1, device_id={"ctx": c - 1}, device_id_type=MESH)

    @pl.when(c < n - 1)
    def _():
        pl.semaphore_signal(barrier, inc=1, device_id={"ctx": c + 1}, device_id_type=MESH)

    step = 16
    own_at = pl.multiple_of(w * feats, feats)
    send_at = pl.multiple_of((1 - w) * feats + s * part, part)

    def normalise(i, carry):
        at = pl.ds(pl.multiple_of(i * step, step), step)
        whole = tokens[at, :].astype(jnp.float32)
        scale = lax.rsqrt(jnp.mean(whole * whole, axis=1, keepdims=True) + epsilon)
        x_send[at, :] = (tokens[at, pl.ds(send_at, part)].astype(jnp.float32) * scale).astype(
            jnp.bfloat16
        )
        x_own[at, :] = (tokens[at, pl.ds(own_at, feats)].astype(jnp.float32) * scale).astype(
            jnp.bfloat16
        )
        return carry

    x_copies = []
    for j in range(ROW_CHUNKS):
        token_loads[j].wait()
        lax.fori_loop(j * (chunk // step), (j + 1) * (chunk // step), normalise, 0)
        if j == 0:
            pl.semaphore_wait(
                barrier, 3 + jnp.minimum(c, 1) + jnp.minimum(n - 1 - c, 1)
            )

        copy = pltpu.make_async_remote_copy(
            src_ref=x_send.at[pl.ds(j * chunk, chunk)],
            dst_ref=x_recv.at[s, pl.ds(j * chunk, chunk)],
            send_sem=xs_sem.at[j],
            recv_sem=xr_sem.at[j],
            device_id=partner,
            device_id_type=MESH,
        )
        copy.start()
        x_copies.append(copy)

    forwards = []

    def forward(j):
        x_copies[j].wait_recv()
        copy = pltpu.make_async_remote_copy(
            src_ref=x_recv.at[s, pl.ds(j * chunk, chunk)],
            dst_ref=x_recv.at[s, pl.ds(j * chunk, chunk)],
            send_sem=fs_sem.at[j],
            recv_sem=fr_sem.at[j],
            device_id=sibling,
            device_id_type=MESH,
        )
        copy.start()
        forwards.append(copy)

    block_len = rows // 2
    q_row = lax.broadcasted_iota(jnp.int32, (2 * rows, 1), 0)
    q_pos = q_row % block_len
    for k in range(4):
        here = q_row // block_len == k
        q_pos = q_pos + jnp.where(here, order[c * 4 + k] * block_len, 0)
    k_col = lax.broadcasted_iota(jnp.int32, (1, 2 * rows * n), 1)
    k_pos = k_col % block_len
    for k in range(4 * n):
        k_pos = k_pos + jnp.where(k_col // block_len == k, order[k] * block_len, 0)
    low = lax.broadcasted_iota(jnp.int32, (rows, hd), 1) < hd // 2
    for b in range(2):
        angles = q_pos[b * rows : (b + 1) * rows].astype(jnp.float32) * freq[...]
        cosine[b] = jnp.cos(angles)
        turn = jnp.sin(angles)
        sine[b] = jnp.where(low, -turn, turn)
    forward(0)

    loads[0].wait()
    kv_wide[...] = kv_raw[...].astype(jnp.float32)
    for h in range(2):
        for t in range(2):
            kv_w[h, :, t * hd : (t + 1) * hd] = kv_wide[
                pl.ds(h * 2 + t, feats, stride=4), :
            ].astype(jnp.bfloat16)
    forward(1)

    def send_part(index, src, dst, block):
        copy = pltpu.make_async_remote_copy(
            src_ref=src.at[block],
            dst_ref=dst.at[block],
            send_sem=ps_sem.at[index],
            recv_sem=pr_sem.at[index],
            device_id=partner,
            device_id_type=MESH,
        )
        copy.start()
        return copy

    f32 = jnp.float32
    own = x_own[...]
    pkv_send[w] = jnp.dot(own, kv_w[1 - w], preferred_element_type=f32).astype(jnp.bfloat16)
    kv_keep[w] = jnp.dot(own, kv_w[w], preferred_element_type=f32)
    forward(2)
    loads[1].wait()
    pq_send[w] = jnp.dot(own, q_w[0], preferred_element_type=f32).astype(jnp.bfloat16)
    forward(3)
    for copy in x_copies:
        copy.wait_send()
    parts = [send_part(0, pkv_send, pkv_recv, w)]
    for copy in forwards:
        copy.wait()

    def other(weight):
        return jnp.dot(x_recv[0], weight[:part], preferred_element_type=f32) + jnp.dot(
            x_recv[1], weight[part:], preferred_element_type=f32
        )

    pkv_send[1 - w] = other(kv_w[1 - w]).astype(jnp.bfloat16)
    parts.append(send_part(1, pkv_send, pkv_recv, 1 - w))
    kv_keep[1 - w] = other(kv_w[w])

    def rotate(t, block):
        turned = pltpu.roll(t, hd // 2, 1)
        return (t * cosine[block] + turned * sine[block]).astype(jnp.bfloat16)

    def z_copy(way, t, b):
        block = c - t if way == 0 else c + t
        at = pl.ds(pl.multiple_of(block * 2 * rows + b * rows, rows), rows)
        return pltpu.make_async_remote_copy(
            src_ref=kv_all.at[at],
            dst_ref=kv_all.at[at],
            send_sem=zs_sem.at[way, t, b],
            recv_sem=zr_sem.at[way, t, b],
            device_id={"ctx": c + 1 if way == 0 else c - 1},
            device_id_type=MESH,
        )

    def z_sends(way, t):
        if way == 0:
            return jnp.logical_and(c - t >= 0, c < n - 1)
        return jnp.logical_and(c + t <= n - 1, c > 0)

    def z_gets(way, t):
        return c - 1 - t >= 0 if way == 0 else c + 1 + t <= n - 1

    for b, index in ((1 - w, 0), (w, 1)):
        parts[index].wait_recv()
        kv = kv_keep[b] + pkv_recv[b].astype(f32)
        at = pl.ds(pl.multiple_of(c * 2 * rows + b * rows, rows), rows)
        kv_all[at, :hd] = rotate(kv[:, :hd], b)
        kv_all[at, hd:] = kv[:, hd:].astype(jnp.bfloat16)
        for way in range(2):

            @pl.when(z_sends(way, 0))
            def _():
                z_copy(way, 0, b).start()

    parts.append(send_part(2, pq_send, pq_recv, w))
    pq_send[1 - w] = other(q_w[0]).astype(jnp.bfloat16)
    parts.append(send_part(3, pq_send, pq_recv, 1 - w))
    loads[2].wait()
    q_keep[w] = jnp.dot(own, q_w[1], preferred_element_type=f32)
    q_keep[1 - w] = other(q_w[1])

    for t in range(n - 1):
        for b in (1 - w, w):
            for way in range(2):

                @pl.when(z_gets(way, t))
                def _():
                    z_copy(way, t, b).wait_recv()

                if t < n - 2:

                    @pl.when(z_sends(way, t + 1))
                    def _():
                        z_copy(way, t + 1, b).start()

    for b, index in ((1 - w, 2), (w, 3)):
        parts[index].wait_recv()
        q = q_keep[b] + pq_recv[b].astype(f32)
        at = pl.ds(pl.multiple_of(b * rows, rows), rows)
        for h in range(heads_here):
            q_rot[h, at, :] = rotate(q[:, h * hd : (h + 1) * hd], b)

    h_copies = []
    factor = 1.0 / hd**0.5
    for h in range(heads_here):
        visible = q_pos >= k_pos
        scores = (
            lax.dot_general(
                q_rot[h], kv_all[:, :hd], (((1,), (1,)), ((), ())), preferred_element_type=f32
            )
            * factor
        )
        scores = jnp.where(visible, scores, -1e30)
        top = jnp.max(scores, axis=1, keepdims=True)
        weights = jnp.where(visible, jnp.exp(scores - top), 0.0)
        total = jnp.sum(weights, axis=1, keepdims=True)
        mixed = jnp.dot(weights.astype(jnp.bfloat16), kv_all[:, hd:], preferred_element_type=f32)
        heads[w, h // 2, :, (h % 2) * hd : (h % 2 + 1) * hd] = (mixed / total).astype(jnp.bfloat16)
        place = heads.at[w, h // 2, :, pl.ds((h % 2) * hd, hd)]
        copy = pltpu.make_async_remote_copy(
            src_ref=place,
            dst_ref=place,
            send_sem=hs_sem.at[h],
            recv_sem=hr_sem.at[h],
            device_id=partner,
            device_id_type=MESH,
        )
        copy.start()
        h_copies.append(copy)
    loads[3].wait()
    for copy in h_copies:
        copy.wait_recv()

    span = o_w.shape[1] // OUT_CHUNKS

    def project(block, j):
        at = pl.ds(pl.multiple_of(block * rows, rows), rows)
        total = None
        for g in range(2):
            for p in range(heads_here // 2):
                first = (g * (heads_here // 2) + p) * 2 * hd
                term = jnp.dot(
                    heads[g, p, at, :],
                    o_w[first : first + 2 * hd, j * span : (j + 1) * span],
                    preferred_element_type=f32,
                )
                total = term if total is None else total + term
        return total

    def o_copy(j):
        return pltpu.make_async_remote_copy(
            src_ref=o_send.at[j],
            dst_ref=o_recv.at[j],
            send_sem=os_sem.at[j],
            recv_sem=or_sem.at[j],
            device_id=sibling,
            device_id_type=MESH,
        )

    def last_copy(j):
        return pltpu.make_async_remote_copy(
            src_ref=o_fin.at[j],
            dst_ref=o_last.at[j],
            send_sem=ls_sem.at[j],
            recv_sem=lr_sem.at[j],
            device_id=across,
            device_id_type=MESH,
        )

    for j in range(OUT_CHUNKS):
        o_keep[...] = project(1 - w, j)

        @pl.when(s == w)
        def _():
            o_send[j] = o_keep[...].astype(jnp.bfloat16)
            o_copy(j).start()

        @pl.when(s != w)
        def _():
            o_copy(j).wait_recv()
            o_fin[j] = (o_keep[...] + o_recv[j].astype(f32)).astype(jnp.bfloat16)
            last_copy(j).start()

    for j in range(OUT_CHUNKS):
        o_keep[...] = project(w, j)

        @pl.when(s != w)
        def _():
            o_send[j] = o_keep[...].astype(jnp.bfloat16)
            o_copy(j).start()

        @pl.when(s == w)
        def _():
            o_copy(j).wait_recv()
            out[:, j * span : (j + 1) * span] = (o_keep[...] + o_recv[j].astype(f32)).astype(
                jnp.bfloat16
            )

    for j in range(OUT_CHUNKS):

        @pl.when(s != w)
        def _():
            last_copy(j).wait()
            out[:, j * span : (j + 1) * span] = o_last[j]

        o_copy(j).wait_send()

    for copy in parts + h_copies:
        copy.wait_send()
    for t in range(n - 1):
        for b in (1 - w, w):
            for way in range(2):

                @pl.when(z_sends(way, t))
                def _():
                    z_copy(way, t, b).wait_send()


def fused_body(n, tokens, block_order, q_weight, key_value_weight, out_weight):
    rows, width = tokens.shape
    feats, kv_local, _, hd = key_value_weight.shape
    q_half = q_weight.shape[1] // 2
    block_len = rows // 2
    steps = np.arange(hd // 2) * 2.0 / hd
    freq = np.tile(rope_base ** (-steps), 2)[None].astype(np.float32)
    bf16, f32 = jnp.bfloat16, jnp.float32
    span = out_weight.shape[1] // OUT_CHUNKS
    here = q_half // hd
    dma = pltpu.SemaphoreType.DMA
    vmem = pl.BlockSpec(memory_space=pltpu.VMEM)
    smem = pl.BlockSpec(memory_space=pltpu.SMEM)
    hbm = pl.BlockSpec(memory_space=pl.ANY)
    return pl.pallas_call(
        functools.partial(fused_kernel, n),
        out_shape=jax.ShapeDtypeStruct((rows, out_weight.shape[1]), bf16),
        in_specs=[hbm, smem, vmem] + [hbm] * 3,
        out_specs=vmem,
        scratch_shapes=[
            pltpu.VMEM(tokens.shape, bf16),
            pltpu.VMEM((2, rows, hd), f32),
            pltpu.VMEM((2, rows, hd), f32),
            pltpu.VMEM((2, feats, q_half), bf16),
            pltpu.VMEM((feats * kv_local * 2, hd), bf16),
            pltpu.VMEM((feats * kv_local * 2, hd), f32),
            pltpu.VMEM((2, feats, 2 * hd), bf16),
            pltpu.VMEM(out_weight.shape, bf16),
            pltpu.VMEM((rows, feats), bf16),
            pltpu.VMEM((rows, feats // 2), bf16),
            pltpu.VMEM((2, rows, feats // 2), bf16),
            pltpu.VMEM((2, rows, 2 * hd), bf16),
            pltpu.VMEM((2, rows, 2 * hd), bf16),
            pltpu.VMEM((2, rows, q_half), bf16),
            pltpu.VMEM((2, rows, q_half), bf16),
            pltpu.VMEM((2, rows, 2 * hd), f32),
            pltpu.VMEM((2, rows, q_half), f32),
            pltpu.VMEM((here, 2 * rows, hd), bf16),
            pltpu.VMEM((n * 2 * rows, 2 * hd), bf16),
            pltpu.VMEM((2, here // 2, 2 * rows, 2 * hd), bf16),
            pltpu.VMEM((rows, span), f32),
            pltpu.VMEM((OUT_CHUNKS, rows, span), bf16),
            pltpu.VMEM((OUT_CHUNKS, rows, span), bf16),
            pltpu.VMEM((OUT_CHUNKS, rows, span), bf16),
            pltpu.VMEM((OUT_CHUNKS, rows, span), bf16),
            dma((ROW_CHUNKS,)),
            dma((4,)),
            dma((ROW_CHUNKS,)),
            dma((ROW_CHUNKS,)),
            dma((ROW_CHUNKS,)),
            dma((ROW_CHUNKS,)),
            dma((4,)),
            dma((4,)),
            dma((2, n - 1, 2)),
            dma((2, n - 1, 2)),
            dma((here,)),
            dma((here,)),
            dma((OUT_CHUNKS,)),
            dma((OUT_CHUNKS,)),
            dma((OUT_CHUNKS,)),
            dma((OUT_CHUNKS,)),
        ],
        compiler_params=pltpu.CompilerParams(
            collective_id=0, has_side_effects=True, vmem_limit_bytes=56 * 1024 * 1024
        ),
    )(
        tokens,
        block_order,
        jnp.asarray(freq),
        q_weight,
        key_value_weight.reshape(feats * kv_local * 2, hd),
        out_weight,
    )


def solution(mesh):
    in_specs = (
        P(("parts", "ctx", "wt"), None),
        P("parts"),
        P("wt", "sub"),
        P("wt", "sub", None, None),
        P("sub", "wt"),
    )
    out_specs = P(("parts", "ctx", "wt"), "sub")
    n = mesh.shape["ctx"]
    fits = mesh.shape["wt"] == 2 and mesh.shape["sub"] == 2 and 1 < n <= 8
    run = functools.partial(fused_body, n) if fits else body
    return jax.shard_map(run, mesh=mesh, in_specs=in_specs, out_specs=out_specs, check_vma=False)
```

```python
import functools

import jax
import jax.numpy as jnp
import numpy as np
from jax import lax
from jax.experimental import pallas as pl
from jax.experimental.pallas import tpu as pltpu
from jax.sharding import PartitionSpec as P

MESH = pl.DeviceIdType.MESH

rope_base = 500000.0
epsilon = 1e-05


def token_positions(row_ids, block_order, block_len):
    number = block_order.shape[0]
    blocks = row_ids // block_len
    equal = blocks[:, None] == jnp.arange(number, dtype=jnp.int32)[None, :]
    chosen = jnp.sum(jnp.where(equal, block_order[None, :], 0), axis=1)
    return chosen * block_len + row_ids % block_len


def rotary(values_in, positions, head_dim):
    half_dim = head_dim // 2
    inverse_freq = rope_base ** (-(jnp.arange(half_dim, dtype=jnp.float32) * 2.0 / head_dim))
    angles = positions.astype(jnp.float32)[:, None] * inverse_freq[None, :]
    cosine = jnp.concatenate([jnp.cos(angles), jnp.cos(angles)], axis=1)[:, None, :]
    sine = jnp.concatenate([jnp.sin(angles), jnp.sin(angles)], axis=1)[:, None, :]
    rotated = jnp.concatenate([-values_in[..., half_dim:], values_in[..., :half_dim]], axis=-1)
    return values_in * cosine + rotated * sine


def body(tokens, block_order, q_weight, key_value_weight, out_weight):
    tok_rows = tokens.shape[0]
    block_len = tok_rows // 2
    head_dim = key_value_weight.shape[3]
    kv_local = key_value_weight.shape[1]
    q_cols = q_weight.shape[1]
    q_local = q_cols // head_dim
    group = q_local // kv_local
    kv_cols = kv_local * 2 * head_dim
    kv_flat = key_value_weight.reshape(key_value_weight.shape[0], kv_cols)
    own_first = lax.axis_index(("ctx", "wt")) * tok_rows
    own_ids = own_first + jnp.arange(tok_rows, dtype=jnp.int32)
    own_positions = token_positions(own_ids, block_order, block_len)
    widened = tokens.astype(jnp.float32)
    normalized_input = (
        widened * lax.rsqrt(jnp.mean(widened * widened, axis=1, keepdims=True) + epsilon)
    ).astype(jnp.bfloat16)
    queries = jnp.dot(
        normalized_input,
        lax.all_gather(q_weight, "wt", axis=0, tiled=True),
        preferred_element_type=jnp.float32,
    )
    key_value_rows = jnp.dot(
        normalized_input,
        lax.all_gather(kv_flat, "wt", axis=0, tiled=True),
        preferred_element_type=jnp.float32,
    )
    queries = queries.reshape(tok_rows, q_local, head_dim)
    key_value_rows = key_value_rows.reshape(tok_rows, kv_local, 2, head_dim)
    q_rot = rotary(queries, own_positions, head_dim).astype(jnp.bfloat16)
    k_rot = rotary(key_value_rows[:, :, 0, :], own_positions, head_dim).astype(jnp.bfloat16)
    value_rows = key_value_rows[:, :, 1, :].astype(jnp.bfloat16)
    q_grouped = jnp.transpose(q_rot.reshape(tok_rows, kv_local, group, head_dim), (1, 2, 0, 3))
    q_grouped = q_grouped.reshape(kv_local, group * tok_rows, head_dim)
    query_positions = jnp.tile(own_positions, group)
    score_factor = 1.0 / head_dim**0.5
    key_part = lax.all_gather(k_rot, ("ctx", "wt"), axis=0, tiled=True)
    value_part = lax.all_gather(value_rows, ("ctx", "wt"), axis=0, tiled=True)
    count = key_part.shape[0]
    key_ids = jnp.arange(count, dtype=jnp.int32)
    key_positions = token_positions(key_ids, block_order, block_len)
    visible = query_positions[:, None] >= key_positions[None, :]
    old_max = jnp.full((kv_local, group * tok_rows), -1e30, jnp.float32)
    scores = (
        jnp.einsum("hqd,khd->hqk", q_grouped, key_part, preferred_element_type=jnp.float32)
        * score_factor
    )
    scores = jnp.where(visible[None], scores, -1e30)
    new_max = jnp.maximum(old_max, jnp.max(scores, axis=2))
    weights = jnp.where(visible[None], jnp.exp(scores - new_max[..., None]), 0.0)
    new_total = jnp.sum(weights, axis=2)
    new_acc = jnp.einsum(
        "hqk,khd->hqd", weights.astype(jnp.bfloat16), value_part, preferred_element_type=jnp.float32
    )
    heads_out = new_acc / new_total[..., None]
    heads_out = jnp.transpose(heads_out.reshape(kv_local, group, tok_rows, head_dim), (2, 0, 1, 3))
    heads_out = heads_out.reshape(tok_rows, q_cols).astype(jnp.bfloat16)
    partial_out = jnp.dot(
        heads_out,
        lax.all_gather(out_weight, "wt", axis=1, tiled=True),
        preferred_element_type=jnp.float32,
    )
    return lax.psum_scatter(
        partial_out.astype(jnp.bfloat16), "sub", scatter_dimension=1, tiled=True
    )


OUT_CHUNKS = 4
ROW_CHUNKS = 4


def fused_kernel(
    n,
    token_hbm,
    order,
    freq,
    q_hbm,
    kv_hbm,
    o_hbm,
    out,
    tokens,
    cosine,
    sine,
    q_w,
    kv_raw,
    kv_wide,
    kv_w,
    o_w,
    x_own,
    x_send,
    x_recv,
    pkv_send,
    pkv_recv,
    pq_send,
    pq_recv,
    kv_keep,
    q_keep,
    q_rot,
    kv_all,
    heads,
    o_keep,
    o_send,
    o_recv,
    o_fin,
    o_last,
    token_sem,
    load_sem,
    xs_sem,
    xr_sem,
    fs_sem,
    fr_sem,
    ps_sem,
    pr_sem,
    zs_sem,
    zr_sem,
    hs_sem,
    hr_sem,
    os_sem,
    or_sem,
    ls_sem,
    lr_sem,
):
    c = lax.axis_index("ctx")
    w = lax.axis_index("wt")
    s = lax.axis_index("sub")
    rows, width = tokens.shape
    feats = width // 2
    part = feats // 2
    hd = 128
    q_half = q_w.shape[2]
    heads_here = q_half // hd
    partner = {"wt": 1 - w}
    sibling = {"sub": 1 - s}
    across = {"wt": 1 - w, "sub": 1 - s}

    chunk = rows // ROW_CHUNKS
    token_loads = [
        pltpu.make_async_copy(
            token_hbm.at[pl.ds(j * chunk, chunk)],
            tokens.at[pl.ds(j * chunk, chunk)],
            token_sem.at[j],
        )
        for j in range(ROW_CHUNKS)
    ]
    for load in token_loads:
        load.start()
    loads = [
        pltpu.make_async_copy(kv_hbm, kv_raw, load_sem.at[0]),
        pltpu.make_async_copy(
            q_hbm.at[:, pl.ds(pl.multiple_of((1 - w) * q_half, q_half), q_half)],
            q_w.at[0],
            load_sem.at[1],
        ),
        pltpu.make_async_copy(
            q_hbm.at[:, pl.ds(pl.multiple_of(w * q_half, q_half), q_half)],
            q_w.at[1],
            load_sem.at[2],
        ),
        pltpu.make_async_copy(o_hbm, o_w, load_sem.at[3]),
    ]
    for load in loads:
        load.start()

    barrier = pltpu.get_barrier_semaphore()
    for target in (partner, sibling, across):
        pl.semaphore_signal(barrier, inc=1, device_id=target, device_id_type=MESH)

    reach = min(2, n - 1)
    for d in range(1, reach + 1):

        @pl.when(c >= d)
        def _():
            pl.semaphore_signal(barrier, inc=1, device_id={"ctx": c - d}, device_id_type=MESH)

        @pl.when(c < n - d)
        def _():
            pl.semaphore_signal(barrier, inc=1, device_id={"ctx": c + d}, device_id_type=MESH)

    step = 16
    own_at = pl.multiple_of(w * feats, feats)
    send_at = pl.multiple_of((1 - w) * feats + s * part, part)

    def normalise(i, carry):
        at = pl.ds(pl.multiple_of(i * step, step), step)
        whole = tokens[at, :].astype(jnp.float32)
        scale = lax.rsqrt(jnp.mean(whole * whole, axis=1, keepdims=True) + epsilon)
        x_send[at, :] = (tokens[at, pl.ds(send_at, part)].astype(jnp.float32) * scale).astype(
            jnp.bfloat16
        )
        x_own[at, :] = (tokens[at, pl.ds(own_at, feats)].astype(jnp.float32) * scale).astype(
            jnp.bfloat16
        )
        return carry

    x_copies = []
    for j in range(ROW_CHUNKS):
        token_loads[j].wait()
        lax.fori_loop(j * (chunk // step), (j + 1) * (chunk // step), normalise, 0)
        if j == 0:
            pl.semaphore_wait(
                barrier, 3 + jnp.minimum(c, reach) + jnp.minimum(n - 1 - c, reach)
            )

        copy = pltpu.make_async_remote_copy(
            src_ref=x_send.at[pl.ds(j * chunk, chunk)],
            dst_ref=x_recv.at[s, pl.ds(j * chunk, chunk)],
            send_sem=xs_sem.at[j],
            recv_sem=xr_sem.at[j],
            device_id=partner,
            device_id_type=MESH,
        )
        copy.start()
        x_copies.append(copy)

    forwards = []

    def forward(j):
        x_copies[j].wait_recv()
        copy = pltpu.make_async_remote_copy(
            src_ref=x_recv.at[s, pl.ds(j * chunk, chunk)],
            dst_ref=x_recv.at[s, pl.ds(j * chunk, chunk)],
            send_sem=fs_sem.at[j],
            recv_sem=fr_sem.at[j],
            device_id=sibling,
            device_id_type=MESH,
        )
        copy.start()
        forwards.append(copy)

    block_len = rows // 2
    q_row = lax.broadcasted_iota(jnp.int32, (2 * rows, 1), 0)
    q_pos = q_row % block_len
    for k in range(4):
        here = q_row // block_len == k
        q_pos = q_pos + jnp.where(here, order[c * 4 + k] * block_len, 0)
    k_col = lax.broadcasted_iota(jnp.int32, (1, 2 * rows * n), 1)
    k_pos = k_col % block_len
    for k in range(4 * n):
        k_pos = k_pos + jnp.where(k_col // block_len == k, order[k] * block_len, 0)
    low = lax.broadcasted_iota(jnp.int32, (rows, hd), 1) < hd // 2
    for b in range(2):
        angles = q_pos[b * rows : (b + 1) * rows].astype(jnp.float32) * freq[...]
        cosine[b] = jnp.cos(angles)
        turn = jnp.sin(angles)
        sine[b] = jnp.where(low, -turn, turn)
    forward(0)

    loads[0].wait()
    kv_wide[...] = kv_raw[...].astype(jnp.float32)
    for h in range(2):
        for t in range(2):
            kv_w[h, :, t * hd : (t + 1) * hd] = kv_wide[
                pl.ds(h * 2 + t, feats, stride=4), :
            ].astype(jnp.bfloat16)
    forward(1)

    def send_part(index, src, dst, block):
        copy = pltpu.make_async_remote_copy(
            src_ref=src.at[block],
            dst_ref=dst.at[block],
            send_sem=ps_sem.at[index],
            recv_sem=pr_sem.at[index],
            device_id=partner,
            device_id_type=MESH,
        )
        copy.start()
        return copy

    f32 = jnp.float32
    own = x_own[...]
    pkv_send[w] = jnp.dot(own, kv_w[1 - w], preferred_element_type=f32).astype(jnp.bfloat16)
    kv_keep[w] = jnp.dot(own, kv_w[w], preferred_element_type=f32)
    forward(2)
    loads[1].wait()
    pq_send[w] = jnp.dot(own, q_w[0], preferred_element_type=f32).astype(jnp.bfloat16)
    forward(3)
    for copy in x_copies:
        copy.wait_send()
    parts = [send_part(0, pkv_send, pkv_recv, w)]
    for copy in forwards:
        copy.wait()

    def other(weight):
        return jnp.dot(x_recv[0], weight[:part], preferred_element_type=f32) + jnp.dot(
            x_recv[1], weight[part:], preferred_element_type=f32
        )

    pkv_send[1 - w] = other(kv_w[1 - w]).astype(jnp.bfloat16)
    parts.append(send_part(1, pkv_send, pkv_recv, 1 - w))
    kv_keep[1 - w] = other(kv_w[w])

    def rotate(t, block):
        turned = pltpu.roll(t, hd // 2, 1)
        return (t * cosine[block] + turned * sine[block]).astype(jnp.bfloat16)

    def z_copy(way, d, b):
        sign = 1 - 2 * way
        block = c if d < 3 else c - 2 * sign
        at = pl.ds(pl.multiple_of(block * 2 * rows + b * rows, rows), rows)
        return pltpu.make_async_remote_copy(
            src_ref=kv_all.at[at],
            dst_ref=kv_all.at[at],
            send_sem=zs_sem.at[way, d - 1, b],
            recv_sem=zr_sem.at[way, d - 1, b],
            device_id={"ctx": c + sign * (d if d < 3 else 1)},
            device_id_type=MESH,
        )

    def z_sends(way, d):
        if d < 3:
            return c < n - d if way == 0 else c >= d
        if way == 0:
            return jnp.logical_and(c >= 2, c < n - 1)
        return jnp.logical_and(c < n - 2, c > 0)

    def z_gets(way, d):
        return c >= d if way == 0 else c < n - d

    def z_get(way, d, b):
        @pl.when(z_gets(way, d))
        def _():
            z_copy(way, d, b).wait_recv()

    def z_send(way, d, b):
        @pl.when(z_sends(way, d))
        def _():
            z_copy(way, d, b).start()

    for b, index in ((1 - w, 0), (w, 1)):
        parts[index].wait_recv()
        kv = kv_keep[b] + pkv_recv[b].astype(f32)
        at = pl.ds(pl.multiple_of(c * 2 * rows + b * rows, rows), rows)
        kv_all[at, :hd] = rotate(kv[:, :hd], b)
        kv_all[at, hd:] = kv[:, hd:].astype(jnp.bfloat16)
        for d in range(reach, 0, -1):
            for way in range(2):
                z_send(way, d, b)

    parts.append(send_part(2, pq_send, pq_recv, w))
    pq_send[1 - w] = other(q_w[0]).astype(jnp.bfloat16)
    parts.append(send_part(3, pq_send, pq_recv, 1 - w))
    loads[2].wait()
    q_keep[w] = jnp.dot(own, q_w[1], preferred_element_type=f32)
    q_keep[1 - w] = other(q_w[1])

    if n > 2:
        for b in (1 - w, w):
            for way in range(2):
                z_get(way, 2, b)
                if n > 3:
                    z_send(way, 3, b)

    for b, index in ((1 - w, 2), (w, 3)):
        parts[index].wait_recv()
        q = q_keep[b] + pq_recv[b].astype(f32)
        at = pl.ds(pl.multiple_of(b * rows, rows), rows)
        for h in range(heads_here):
            q_rot[h, at, :] = rotate(q[:, h * hd : (h + 1) * hd], b)

    for d in (1, 3):
        if d < n:
            for b in (1 - w, w):
                for way in range(2):
                    z_get(way, d, b)

    h_copies = []
    factor = 1.0 / hd**0.5
    for h in range(heads_here):
        visible = q_pos >= k_pos
        scores = (
            lax.dot_general(
                q_rot[h], kv_all[:, :hd], (((1,), (1,)), ((), ())), preferred_element_type=f32
            )
            * factor
        )
        scores = jnp.where(visible, scores, -1e30)
        top = jnp.max(scores, axis=1, keepdims=True)
        weights = jnp.where(visible, jnp.exp(scores - top), 0.0)
        total = jnp.sum(weights, axis=1, keepdims=True)
        mixed = jnp.dot(weights.astype(jnp.bfloat16), kv_all[:, hd:], preferred_element_type=f32)
        heads[w, h // 2, :, (h % 2) * hd : (h % 2 + 1) * hd] = (mixed / total).astype(jnp.bfloat16)
        place = heads.at[w, h // 2, :, pl.ds((h % 2) * hd, hd)]
        copy = pltpu.make_async_remote_copy(
            src_ref=place,
            dst_ref=place,
            send_sem=hs_sem.at[h],
            recv_sem=hr_sem.at[h],
            device_id=partner,
            device_id_type=MESH,
        )
        copy.start()
        h_copies.append(copy)
    loads[3].wait()
    for copy in h_copies:
        copy.wait_recv()

    span = o_w.shape[1] // OUT_CHUNKS

    def project(block, j):
        at = pl.ds(pl.multiple_of(block * rows, rows), rows)
        total = None
        for g in range(2):
            for p in range(heads_here // 2):
                first = (g * (heads_here // 2) + p) * 2 * hd
                term = jnp.dot(
                    heads[g, p, at, :],
                    o_w[first : first + 2 * hd, j * span : (j + 1) * span],
                    preferred_element_type=f32,
                )
                total = term if total is None else total + term
        return total

    def o_copy(j):
        return pltpu.make_async_remote_copy(
            src_ref=o_send.at[j],
            dst_ref=o_recv.at[j],
            send_sem=os_sem.at[j],
            recv_sem=or_sem.at[j],
            device_id=sibling,
            device_id_type=MESH,
        )

    def last_copy(j):
        return pltpu.make_async_remote_copy(
            src_ref=o_fin.at[j],
            dst_ref=o_last.at[j],
            send_sem=ls_sem.at[j],
            recv_sem=lr_sem.at[j],
            device_id=across,
            device_id_type=MESH,
        )

    for j in range(OUT_CHUNKS):
        o_keep[...] = project(1 - w, j)

        @pl.when(s == w)
        def _():
            o_send[j] = o_keep[...].astype(jnp.bfloat16)
            o_copy(j).start()

        @pl.when(s != w)
        def _():
            o_copy(j).wait_recv()
            o_fin[j] = (o_keep[...] + o_recv[j].astype(f32)).astype(jnp.bfloat16)
            last_copy(j).start()

    for j in range(OUT_CHUNKS):
        o_keep[...] = project(w, j)

        @pl.when(s != w)
        def _():
            o_send[j] = o_keep[...].astype(jnp.bfloat16)
            o_copy(j).start()

        @pl.when(s == w)
        def _():
            o_copy(j).wait_recv()
            out[:, j * span : (j + 1) * span] = (o_keep[...] + o_recv[j].astype(f32)).astype(
                jnp.bfloat16
            )

    for j in range(OUT_CHUNKS):

        @pl.when(s != w)
        def _():
            last_copy(j).wait()
            out[:, j * span : (j + 1) * span] = o_last[j]

        o_copy(j).wait_send()

    for copy in parts + h_copies:
        copy.wait_send()
    for d in range(1, n):
        for b in (1 - w, w):
            for way in range(2):

                @pl.when(z_sends(way, d))
                def _():
                    z_copy(way, d, b).wait_send()


def fused_body(n, tokens, block_order, q_weight, key_value_weight, out_weight):
    rows, width = tokens.shape
    feats, kv_local, _, hd = key_value_weight.shape
    q_half = q_weight.shape[1] // 2
    block_len = rows // 2
    steps = np.arange(hd // 2) * 2.0 / hd
    freq = np.tile(rope_base ** (-steps), 2)[None].astype(np.float32)
    bf16, f32 = jnp.bfloat16, jnp.float32
    span = out_weight.shape[1] // OUT_CHUNKS
    here = q_half // hd
    dma = pltpu.SemaphoreType.DMA
    vmem = pl.BlockSpec(memory_space=pltpu.VMEM)
    smem = pl.BlockSpec(memory_space=pltpu.SMEM)
    hbm = pl.BlockSpec(memory_space=pl.ANY)
    return pl.pallas_call(
        functools.partial(fused_kernel, n),
        out_shape=jax.ShapeDtypeStruct((rows, out_weight.shape[1]), bf16),
        in_specs=[hbm, smem, vmem] + [hbm] * 3,
        out_specs=vmem,
        scratch_shapes=[
            pltpu.VMEM(tokens.shape, bf16),
            pltpu.VMEM((2, rows, hd), f32),
            pltpu.VMEM((2, rows, hd), f32),
            pltpu.VMEM((2, feats, q_half), bf16),
            pltpu.VMEM((feats * kv_local * 2, hd), bf16),
            pltpu.VMEM((feats * kv_local * 2, hd), f32),
            pltpu.VMEM((2, feats, 2 * hd), bf16),
            pltpu.VMEM(out_weight.shape, bf16),
            pltpu.VMEM((rows, feats), bf16),
            pltpu.VMEM((rows, feats // 2), bf16),
            pltpu.VMEM((2, rows, feats // 2), bf16),
            pltpu.VMEM((2, rows, 2 * hd), bf16),
            pltpu.VMEM((2, rows, 2 * hd), bf16),
            pltpu.VMEM((2, rows, q_half), bf16),
            pltpu.VMEM((2, rows, q_half), bf16),
            pltpu.VMEM((2, rows, 2 * hd), f32),
            pltpu.VMEM((2, rows, q_half), f32),
            pltpu.VMEM((here, 2 * rows, hd), bf16),
            pltpu.VMEM((n * 2 * rows, 2 * hd), bf16),
            pltpu.VMEM((2, here // 2, 2 * rows, 2 * hd), bf16),
            pltpu.VMEM((rows, span), f32),
            pltpu.VMEM((OUT_CHUNKS, rows, span), bf16),
            pltpu.VMEM((OUT_CHUNKS, rows, span), bf16),
            pltpu.VMEM((OUT_CHUNKS, rows, span), bf16),
            pltpu.VMEM((OUT_CHUNKS, rows, span), bf16),
            dma((ROW_CHUNKS,)),
            dma((4,)),
            dma((ROW_CHUNKS,)),
            dma((ROW_CHUNKS,)),
            dma((ROW_CHUNKS,)),
            dma((ROW_CHUNKS,)),
            dma((4,)),
            dma((4,)),
            dma((2, n - 1, 2)),
            dma((2, n - 1, 2)),
            dma((here,)),
            dma((here,)),
            dma((OUT_CHUNKS,)),
            dma((OUT_CHUNKS,)),
            dma((OUT_CHUNKS,)),
            dma((OUT_CHUNKS,)),
        ],
        compiler_params=pltpu.CompilerParams(
            collective_id=0, has_side_effects=True, vmem_limit_bytes=56 * 1024 * 1024
        ),
    )(
        tokens,
        block_order,
        jnp.asarray(freq),
        q_weight,
        key_value_weight.reshape(feats * kv_local * 2, hd),
        out_weight,
    )


def solution(mesh):
    in_specs = (
        P(("parts", "ctx", "wt"), None),
        P("parts"),
        P("wt", "sub"),
        P("wt", "sub", None, None),
        P("sub", "wt"),
    )
    out_specs = P(("parts", "ctx", "wt"), "sub")
    n = mesh.shape["ctx"]
    fits = mesh.shape["wt"] == 2 and mesh.shape["sub"] == 2 and 1 < n <= 4
    run = functools.partial(fused_body, n) if fits else body
    return jax.shard_map(run, mesh=mesh, in_specs=in_specs, out_specs=out_specs, check_vma=False)
```

```python
import functools

import jax
import jax.numpy as jnp
import numpy as np
from jax import lax
from jax.experimental import pallas as pl
from jax.experimental.pallas import tpu as pltpu
from jax.sharding import PartitionSpec as P

MESH = pl.DeviceIdType.MESH

rope_base = 500000.0
epsilon = 1e-05


def token_positions(row_ids, block_order, block_len):
    number = block_order.shape[0]
    blocks = row_ids // block_len
    equal = blocks[:, None] == jnp.arange(number, dtype=jnp.int32)[None, :]
    chosen = jnp.sum(jnp.where(equal, block_order[None, :], 0), axis=1)
    return chosen * block_len + row_ids % block_len


def rotary(values_in, positions, head_dim):
    half_dim = head_dim // 2
    inverse_freq = rope_base ** (-(jnp.arange(half_dim, dtype=jnp.float32) * 2.0 / head_dim))
    angles = positions.astype(jnp.float32)[:, None] * inverse_freq[None, :]
    cosine = jnp.concatenate([jnp.cos(angles), jnp.cos(angles)], axis=1)[:, None, :]
    sine = jnp.concatenate([jnp.sin(angles), jnp.sin(angles)], axis=1)[:, None, :]
    rotated = jnp.concatenate([-values_in[..., half_dim:], values_in[..., :half_dim]], axis=-1)
    return values_in * cosine + rotated * sine


def body(tokens, block_order, q_weight, key_value_weight, out_weight):
    tok_rows = tokens.shape[0]
    block_len = tok_rows // 2
    head_dim = key_value_weight.shape[3]
    kv_local = key_value_weight.shape[1]
    q_cols = q_weight.shape[1]
    q_local = q_cols // head_dim
    group = q_local // kv_local
    kv_cols = kv_local * 2 * head_dim
    kv_flat = key_value_weight.reshape(key_value_weight.shape[0], kv_cols)
    own_first = lax.axis_index(("ctx", "wt")) * tok_rows
    own_ids = own_first + jnp.arange(tok_rows, dtype=jnp.int32)
    own_positions = token_positions(own_ids, block_order, block_len)
    widened = tokens.astype(jnp.float32)
    normalized_input = (
        widened * lax.rsqrt(jnp.mean(widened * widened, axis=1, keepdims=True) + epsilon)
    ).astype(jnp.bfloat16)
    queries = jnp.dot(
        normalized_input,
        lax.all_gather(q_weight, "wt", axis=0, tiled=True),
        preferred_element_type=jnp.float32,
    )
    key_value_rows = jnp.dot(
        normalized_input,
        lax.all_gather(kv_flat, "wt", axis=0, tiled=True),
        preferred_element_type=jnp.float32,
    )
    queries = queries.reshape(tok_rows, q_local, head_dim)
    key_value_rows = key_value_rows.reshape(tok_rows, kv_local, 2, head_dim)
    q_rot = rotary(queries, own_positions, head_dim).astype(jnp.bfloat16)
    k_rot = rotary(key_value_rows[:, :, 0, :], own_positions, head_dim).astype(jnp.bfloat16)
    value_rows = key_value_rows[:, :, 1, :].astype(jnp.bfloat16)
    q_grouped = jnp.transpose(q_rot.reshape(tok_rows, kv_local, group, head_dim), (1, 2, 0, 3))
    q_grouped = q_grouped.reshape(kv_local, group * tok_rows, head_dim)
    query_positions = jnp.tile(own_positions, group)
    score_factor = 1.0 / head_dim**0.5
    key_part = lax.all_gather(k_rot, ("ctx", "wt"), axis=0, tiled=True)
    value_part = lax.all_gather(value_rows, ("ctx", "wt"), axis=0, tiled=True)
    count = key_part.shape[0]
    key_ids = jnp.arange(count, dtype=jnp.int32)
    key_positions = token_positions(key_ids, block_order, block_len)
    visible = query_positions[:, None] >= key_positions[None, :]
    old_max = jnp.full((kv_local, group * tok_rows), -1e30, jnp.float32)
    scores = (
        jnp.einsum("hqd,khd->hqk", q_grouped, key_part, preferred_element_type=jnp.float32)
        * score_factor
    )
    scores = jnp.where(visible[None], scores, -1e30)
    new_max = jnp.maximum(old_max, jnp.max(scores, axis=2))
    weights = jnp.where(visible[None], jnp.exp(scores - new_max[..., None]), 0.0)
    new_total = jnp.sum(weights, axis=2)
    new_acc = jnp.einsum(
        "hqk,khd->hqd", weights.astype(jnp.bfloat16), value_part, preferred_element_type=jnp.float32
    )
    heads_out = new_acc / new_total[..., None]
    heads_out = jnp.transpose(heads_out.reshape(kv_local, group, tok_rows, head_dim), (2, 0, 1, 3))
    heads_out = heads_out.reshape(tok_rows, q_cols).astype(jnp.bfloat16)
    partial_out = jnp.dot(
        heads_out,
        lax.all_gather(out_weight, "wt", axis=1, tiled=True),
        preferred_element_type=jnp.float32,
    )
    return lax.psum_scatter(
        partial_out.astype(jnp.bfloat16), "sub", scatter_dimension=1, tiled=True
    )


OUT_CHUNKS = 4
ROW_CHUNKS = 4


def fused_kernel(
    n,
    token_hbm,
    order,
    freq,
    q_hbm,
    kv_hbm,
    o_hbm,
    out,
    tokens,
    cosine,
    sine,
    q_w,
    kv_raw,
    kv_wide,
    kv_w,
    o_w,
    x_own,
    x_send,
    x_recv,
    pkv_send,
    pkv_recv,
    pq_send,
    pq_recv,
    kv_keep,
    q_keep,
    q_rot,
    kv_all,
    heads,
    o_keep,
    o_send,
    o_recv,
    o_fin,
    o_last,
    token_sem,
    load_sem,
    xs_sem,
    xr_sem,
    fs_sem,
    fr_sem,
    ps_sem,
    pr_sem,
    zs_sem,
    zr_sem,
    hs_sem,
    hr_sem,
    os_sem,
    or_sem,
    ls_sem,
    lr_sem,
):
    c = lax.axis_index("ctx")
    w = lax.axis_index("wt")
    s = lax.axis_index("sub")
    rows, width = tokens.shape
    feats = width // 2
    part = feats // 2
    hd = 128
    q_half = q_w.shape[2]
    heads_here = q_half // hd
    partner = {"wt": 1 - w}
    sibling = {"sub": 1 - s}
    across = {"wt": 1 - w, "sub": 1 - s}

    chunk = rows // ROW_CHUNKS
    token_loads = [
        pltpu.make_async_copy(
            token_hbm.at[pl.ds(j * chunk, chunk)],
            tokens.at[pl.ds(j * chunk, chunk)],
            token_sem.at[j],
        )
        for j in range(ROW_CHUNKS)
    ]
    for load in token_loads:
        load.start()
    loads = [
        pltpu.make_async_copy(kv_hbm, kv_raw, load_sem.at[0]),
        pltpu.make_async_copy(
            q_hbm.at[:, pl.ds(pl.multiple_of((1 - w) * q_half, q_half), q_half)],
            q_w.at[0],
            load_sem.at[1],
        ),
        pltpu.make_async_copy(
            q_hbm.at[:, pl.ds(pl.multiple_of(w * q_half, q_half), q_half)],
            q_w.at[1],
            load_sem.at[2],
        ),
        pltpu.make_async_copy(o_hbm, o_w, load_sem.at[3]),
    ]
    for load in loads:
        load.start()

    barrier = pltpu.get_barrier_semaphore()
    for target in (partner, sibling, across):
        pl.semaphore_signal(barrier, inc=1, device_id=target, device_id_type=MESH)

    reach = min(2, n - 1)
    for d in range(1, reach + 1):

        @pl.when(c >= d)
        def _():
            pl.semaphore_signal(barrier, inc=1, device_id={"ctx": c - d}, device_id_type=MESH)

        @pl.when(c < n - d)
        def _():
            pl.semaphore_signal(barrier, inc=1, device_id={"ctx": c + d}, device_id_type=MESH)

    step = 16
    own_at = pl.multiple_of(w * feats, feats)
    send_at = pl.multiple_of((1 - w) * feats + s * part, part)

    def normalise(i, carry):
        at = pl.ds(pl.multiple_of(i * step, step), step)
        whole = tokens[at, :].astype(jnp.float32)
        scale = lax.rsqrt(jnp.mean(whole * whole, axis=1, keepdims=True) + epsilon)
        x_send[at, :] = (tokens[at, pl.ds(send_at, part)].astype(jnp.float32) * scale).astype(
            jnp.bfloat16
        )
        x_own[at, :] = (tokens[at, pl.ds(own_at, feats)].astype(jnp.float32) * scale).astype(
            jnp.bfloat16
        )
        return carry

    x_copies = []
    for j in range(ROW_CHUNKS):
        token_loads[j].wait()
        lax.fori_loop(j * (chunk // step), (j + 1) * (chunk // step), normalise, 0)
        if j == 0:
            pl.semaphore_wait(
                barrier, 3 + jnp.minimum(c, reach) + jnp.minimum(n - 1 - c, reach)
            )

        copy = pltpu.make_async_remote_copy(
            src_ref=x_send.at[pl.ds(j * chunk, chunk)],
            dst_ref=x_recv.at[s, pl.ds(j * chunk, chunk)],
            send_sem=xs_sem.at[j],
            recv_sem=xr_sem.at[j],
            device_id=partner,
            device_id_type=MESH,
        )
        copy.start()
        x_copies.append(copy)

    forwards = []

    def forward(j):
        x_copies[j].wait_recv()
        copy = pltpu.make_async_remote_copy(
            src_ref=x_recv.at[s, pl.ds(j * chunk, chunk)],
            dst_ref=x_recv.at[s, pl.ds(j * chunk, chunk)],
            send_sem=fs_sem.at[j],
            recv_sem=fr_sem.at[j],
            device_id=sibling,
            device_id_type=MESH,
        )
        copy.start()
        forwards.append(copy)

    block_len = rows // 2
    q_row = lax.broadcasted_iota(jnp.int32, (2 * rows, 1), 0)
    q_pos = q_row % block_len
    for k in range(4):
        here = q_row // block_len == k
        q_pos = q_pos + jnp.where(here, order[c * 4 + k] * block_len, 0)
    k_col = lax.broadcasted_iota(jnp.int32, (1, 2 * rows * n), 1)
    k_pos = k_col % block_len
    for k in range(4 * n):
        k_pos = k_pos + jnp.where(k_col // block_len == k, order[k] * block_len, 0)
    low = lax.broadcasted_iota(jnp.int32, (rows, hd), 1) < hd // 2
    for b in range(2):
        angles = q_pos[b * rows : (b + 1) * rows].astype(jnp.float32) * freq[...]
        cosine[b] = jnp.cos(angles)
        turn = jnp.sin(angles)
        sine[b] = jnp.where(low, -turn, turn)
    forward(0)

    loads[0].wait()
    kv_wide[...] = kv_raw[...].astype(jnp.float32)
    for h in range(2):
        for t in range(2):
            kv_w[h, :, t * hd : (t + 1) * hd] = kv_wide[
                pl.ds(h * 2 + t, feats, stride=4), :
            ].astype(jnp.bfloat16)
    forward(1)

    def send_part(index, src, dst, block):
        copy = pltpu.make_async_remote_copy(
            src_ref=src.at[block],
            dst_ref=dst.at[block],
            send_sem=ps_sem.at[index],
            recv_sem=pr_sem.at[index],
            device_id=partner,
            device_id_type=MESH,
        )
        copy.start()
        return copy

    f32 = jnp.float32
    own = x_own[...]
    pkv_send[w] = jnp.dot(own, kv_w[1 - w], preferred_element_type=f32).astype(jnp.bfloat16)
    kv_keep[w] = jnp.dot(own, kv_w[w], preferred_element_type=f32)
    forward(2)
    loads[1].wait()
    pq_send[w] = jnp.dot(own, q_w[0], preferred_element_type=f32).astype(jnp.bfloat16)
    forward(3)
    for copy in x_copies:
        copy.wait_send()
    parts = [send_part(0, pkv_send, pkv_recv, w)]
    for copy in forwards:
        copy.wait()

    def other(weight):
        return jnp.dot(x_recv[0], weight[:part], preferred_element_type=f32) + jnp.dot(
            x_recv[1], weight[part:], preferred_element_type=f32
        )

    pkv_send[1 - w] = other(kv_w[1 - w]).astype(jnp.bfloat16)
    parts.append(send_part(1, pkv_send, pkv_recv, 1 - w))
    kv_keep[1 - w] = other(kv_w[w])
    parts.append(send_part(2, pq_send, pq_recv, w))

    def rotate(t, block):
        turned = pltpu.roll(t, hd // 2, 1)
        return (t * cosine[block] + turned * sine[block]).astype(jnp.bfloat16)

    def z_copy(way, d, b):
        sign = 1 - 2 * way
        block = c if d < 3 else c - 2 * sign
        at = pl.ds(pl.multiple_of(block * 2 * rows + b * rows, rows), rows)
        return pltpu.make_async_remote_copy(
            src_ref=kv_all.at[at],
            dst_ref=kv_all.at[at],
            send_sem=zs_sem.at[way, d - 1, b],
            recv_sem=zr_sem.at[way, d - 1, b],
            device_id={"ctx": c + sign * (d if d < 3 else 1)},
            device_id_type=MESH,
        )

    def z_sends(way, d):
        if d < 3:
            return c < n - d if way == 0 else c >= d
        if way == 0:
            return jnp.logical_and(c >= 2, c < n - 1)
        return jnp.logical_and(c < n - 2, c > 0)

    def z_gets(way, d):
        return c >= d if way == 0 else c < n - d

    def z_get(way, d, b):
        @pl.when(z_gets(way, d))
        def _():
            z_copy(way, d, b).wait_recv()

    def z_send(way, d, b):
        @pl.when(z_sends(way, d))
        def _():
            z_copy(way, d, b).start()

    for b, index in ((1 - w, 0), (w, 1)):
        parts[index].wait_recv()
        kv = kv_keep[b] + pkv_recv[b].astype(f32)
        at = pl.ds(pl.multiple_of(c * 2 * rows + b * rows, rows), rows)
        kv_all[at, :hd] = rotate(kv[:, :hd], b)
        kv_all[at, hd:] = kv[:, hd:].astype(jnp.bfloat16)
        for d in range(reach, 0, -1):
            for way in range(2):
                z_send(way, d, b)

    pq_send[1 - w] = other(q_w[0]).astype(jnp.bfloat16)
    parts.append(send_part(3, pq_send, pq_recv, 1 - w))
    loads[2].wait()
    q_keep[w] = jnp.dot(own, q_w[1], preferred_element_type=f32)
    q_keep[1 - w] = other(q_w[1])

    if n > 2:
        for b in (1 - w, w):
            for way in range(2):
                z_get(way, 2, b)
                if n > 3:
                    z_send(way, 3, b)

    for b, index in ((1 - w, 2), (w, 3)):
        parts[index].wait_recv()
        q = q_keep[b] + pq_recv[b].astype(f32)
        at = pl.ds(pl.multiple_of(b * rows, rows), rows)
        for h in range(heads_here):
            q_rot[h, at, :] = rotate(q[:, h * hd : (h + 1) * hd], b)

    for d in (1, 3):
        if d < n:
            for b in (1 - w, w):
                for way in range(2):
                    z_get(way, d, b)

    h_copies = []
    factor = 1.0 / hd**0.5
    for h in range(heads_here):
        visible = q_pos >= k_pos
        scores = (
            lax.dot_general(
                q_rot[h], kv_all[:, :hd], (((1,), (1,)), ((), ())), preferred_element_type=f32
            )
            * factor
        )
        scores = jnp.where(visible, scores, -1e30)
        top = jnp.max(scores, axis=1, keepdims=True)
        weights = jnp.where(visible, jnp.exp(scores - top), 0.0)
        total = jnp.sum(weights, axis=1, keepdims=True)
        mixed = jnp.dot(weights.astype(jnp.bfloat16), kv_all[:, hd:], preferred_element_type=f32)
        heads[w, h // 2, :, (h % 2) * hd : (h % 2 + 1) * hd] = (mixed / total).astype(jnp.bfloat16)
        place = heads.at[w, h // 2, :, pl.ds((h % 2) * hd, hd)]
        copy = pltpu.make_async_remote_copy(
            src_ref=place,
            dst_ref=place,
            send_sem=hs_sem.at[h],
            recv_sem=hr_sem.at[h],
            device_id=partner,
            device_id_type=MESH,
        )
        copy.start()
        h_copies.append(copy)
    loads[3].wait()
    for copy in h_copies:
        copy.wait_recv()

    span = o_w.shape[1] // OUT_CHUNKS

    def project(block, j):
        at = pl.ds(pl.multiple_of(block * rows, rows), rows)
        total = None
        for g in range(2):
            for p in range(heads_here // 2):
                first = (g * (heads_here // 2) + p) * 2 * hd
                term = jnp.dot(
                    heads[g, p, at, :],
                    o_w[first : first + 2 * hd, j * span : (j + 1) * span],
                    preferred_element_type=f32,
                )
                total = term if total is None else total + term
        return total

    def o_copy(j):
        return pltpu.make_async_remote_copy(
            src_ref=o_send.at[j],
            dst_ref=o_recv.at[j],
            send_sem=os_sem.at[j],
            recv_sem=or_sem.at[j],
            device_id=sibling,
            device_id_type=MESH,
        )

    def last_copy(j):
        return pltpu.make_async_remote_copy(
            src_ref=o_fin.at[j],
            dst_ref=o_last.at[j],
            send_sem=ls_sem.at[j],
            recv_sem=lr_sem.at[j],
            device_id=across,
            device_id_type=MESH,
        )

    for j in range(OUT_CHUNKS):
        o_keep[...] = project(1 - w, j)

        @pl.when(s == w)
        def _():
            o_send[j] = o_keep[...].astype(jnp.bfloat16)
            o_copy(j).start()

        @pl.when(s != w)
        def _():
            o_copy(j).wait_recv()
            o_fin[j] = (o_keep[...] + o_recv[j].astype(f32)).astype(jnp.bfloat16)
            last_copy(j).start()

    for j in range(OUT_CHUNKS):
        o_keep[...] = project(w, j)

        @pl.when(s != w)
        def _():
            o_send[j] = o_keep[...].astype(jnp.bfloat16)
            o_copy(j).start()

        @pl.when(s == w)
        def _():
            o_copy(j).wait_recv()
            out[:, j * span : (j + 1) * span] = (o_keep[...] + o_recv[j].astype(f32)).astype(
                jnp.bfloat16
            )

    for j in range(OUT_CHUNKS):

        @pl.when(s != w)
        def _():
            last_copy(j).wait()
            out[:, j * span : (j + 1) * span] = o_last[j]

        o_copy(j).wait_send()

    for copy in parts + h_copies:
        copy.wait_send()
    for d in range(1, n):
        for b in (1 - w, w):
            for way in range(2):

                @pl.when(z_sends(way, d))
                def _():
                    z_copy(way, d, b).wait_send()


def fused_body(n, tokens, block_order, q_weight, key_value_weight, out_weight):
    rows, width = tokens.shape
    feats, kv_local, _, hd = key_value_weight.shape
    q_half = q_weight.shape[1] // 2
    block_len = rows // 2
    steps = np.arange(hd // 2) * 2.0 / hd
    freq = np.tile(rope_base ** (-steps), 2)[None].astype(np.float32)
    bf16, f32 = jnp.bfloat16, jnp.float32
    span = out_weight.shape[1] // OUT_CHUNKS
    here = q_half // hd
    dma = pltpu.SemaphoreType.DMA
    vmem = pl.BlockSpec(memory_space=pltpu.VMEM)
    smem = pl.BlockSpec(memory_space=pltpu.SMEM)
    hbm = pl.BlockSpec(memory_space=pl.ANY)
    return pl.pallas_call(
        functools.partial(fused_kernel, n),
        out_shape=jax.ShapeDtypeStruct((rows, out_weight.shape[1]), bf16),
        in_specs=[hbm, smem, vmem] + [hbm] * 3,
        out_specs=vmem,
        scratch_shapes=[
            pltpu.VMEM(tokens.shape, bf16),
            pltpu.VMEM((2, rows, hd), f32),
            pltpu.VMEM((2, rows, hd), f32),
            pltpu.VMEM((2, feats, q_half), bf16),
            pltpu.VMEM((feats * kv_local * 2, hd), bf16),
            pltpu.VMEM((feats * kv_local * 2, hd), f32),
            pltpu.VMEM((2, feats, 2 * hd), bf16),
            pltpu.VMEM(out_weight.shape, bf16),
            pltpu.VMEM((rows, feats), bf16),
            pltpu.VMEM((rows, feats // 2), bf16),
            pltpu.VMEM((2, rows, feats // 2), bf16),
            pltpu.VMEM((2, rows, 2 * hd), bf16),
            pltpu.VMEM((2, rows, 2 * hd), bf16),
            pltpu.VMEM((2, rows, q_half), bf16),
            pltpu.VMEM((2, rows, q_half), bf16),
            pltpu.VMEM((2, rows, 2 * hd), f32),
            pltpu.VMEM((2, rows, q_half), f32),
            pltpu.VMEM((here, 2 * rows, hd), bf16),
            pltpu.VMEM((n * 2 * rows, 2 * hd), bf16),
            pltpu.VMEM((2, here // 2, 2 * rows, 2 * hd), bf16),
            pltpu.VMEM((rows, span), f32),
            pltpu.VMEM((OUT_CHUNKS, rows, span), bf16),
            pltpu.VMEM((OUT_CHUNKS, rows, span), bf16),
            pltpu.VMEM((OUT_CHUNKS, rows, span), bf16),
            pltpu.VMEM((OUT_CHUNKS, rows, span), bf16),
            dma((ROW_CHUNKS,)),
            dma((4,)),
            dma((ROW_CHUNKS,)),
            dma((ROW_CHUNKS,)),
            dma((ROW_CHUNKS,)),
            dma((ROW_CHUNKS,)),
            dma((4,)),
            dma((4,)),
            dma((2, n - 1, 2)),
            dma((2, n - 1, 2)),
            dma((here,)),
            dma((here,)),
            dma((OUT_CHUNKS,)),
            dma((OUT_CHUNKS,)),
            dma((OUT_CHUNKS,)),
            dma((OUT_CHUNKS,)),
        ],
        compiler_params=pltpu.CompilerParams(
            collective_id=0, has_side_effects=True, vmem_limit_bytes=56 * 1024 * 1024
        ),
    )(
        tokens,
        block_order,
        jnp.asarray(freq),
        q_weight,
        key_value_weight.reshape(feats * kv_local * 2, hd),
        out_weight,
    )


def solution(mesh):
    in_specs = (
        P(("parts", "ctx", "wt"), None),
        P("parts"),
        P("wt", "sub"),
        P("wt", "sub", None, None),
        P("sub", "wt"),
    )
    out_specs = P(("parts", "ctx", "wt"), "sub")
    n = mesh.shape["ctx"]
    fits = mesh.shape["wt"] == 2 and mesh.shape["sub"] == 2 and 1 < n <= 4
    run = functools.partial(fused_body, n) if fits else body
    return jax.shard_map(run, mesh=mesh, in_specs=in_specs, out_specs=out_specs, check_vma=False)
```
